32 devices in a mesh: grp: 2 (over x), tsec: 1, lat: 16 (over z, y, core).
Axes of the slice: x: 2, y: 2, z: 4, core: 2. Of those that a mesh axis runs over, the one named last changes fastest.
Arguments:
- sources: bfloat16 [2048, 1792], P(('grp', 'lat'), 'tsec'), parts along dimension 0, may hold values from -6 to 6
- errors: bfloat16 [1, 2048, 1792], P('tsec', ('grp', 'lat')), parts along dimension 1, may hold values from -6 to 6
- enc_weight: bfloat16 [1792, 8192], P('tsec', 'lat'), may hold values from -0.125 to 0.125
- enc_bias: float32 [8192], P('lat'), may hold values from -3 to 3
- dec_weight: bfloat16 [1, 8192, 1792], P('tsec', 'lat'), may hold values from -0.1875 to 0.1875
- active: int32 [2048, 8192], P('grp', 'lat'), parts along dimension 0, may hold values 0 or 1
Outputs:
- code_grad: float32 [2048, 8192], P(('grp', 'tsec'), 'lat'), parts along dimension 0
- dec_grad: float32 [1, 16384, 1792], P('tsec', ('grp', 'lat')), parts along dimension 1
- enc_grad: float32 [3584, 8192], P(('grp', 'tsec'), 'lat'), parts along dimension 0
- input_grad: float32 [2048, 1792], P(('grp', 'lat'), 'tsec'), parts along dimension 0
The draws below stay inside these ranges and needn't reach their ends.
There are 2 independent parts, one for each index of `grp`. The reference program is written for one: setup_inputs(seed, part) draws one part's arguments, and reference() takes and returns one part's arrays. A program takes and returns all parts, laid end to end along the dimension named above; an argument that names none is the same for every part. Nothing has to cross between parts.
All inputs are finite; a program needn't handle non-finite values. No bound on the sum of `active` on one device may be relied on, other than what follows from the above.
Results may differ from the reference program's by a relative error of at most 0.0029.
Values may be sent and summed in bfloat16 or wider, within the bound.
No kernel may reach another device: no remote copies, remote signals or barrier semaphores. Data moves between devices by JAX's collectives and lax.ppermute only.
A program may use at most 64 MiB of HBM per device.

```python
import jax
import jax.numpy as jnp

D = 1792
TOKENS = 1024
LATENTS = 8192
TARGETS = 1


def touch_ends(values, rng, least, largest):
    extent = values.shape
    spot = [jax.random.randint(jax.random.fold_in(rng, axis), (), 0, extent[axis]) for axis in range(len(extent))]
    values = values.at[tuple(spot)].set(least)
    longest = extent.index(max(extent))
    spot[longest] = (spot[longest] + 1) % extent[longest]
    return values.at[tuple(spot)].set(largest)


def shard_levels(stream_key, extent, cuts, least, high):
    level, own = 1.0, jax.random.fold_in(stream_key, 6)
    for dim, blocks in cuts:
        heights = jnp.exp(jax.random.uniform(jax.random.fold_in(own, dim), (blocks,), jnp.float32, least / len(cuts), high / len(cuts)))
        level = level * jnp.repeat(heights, extent[dim] // blocks).reshape([-1 if axis == dim else 1 for axis in range(len(extent))])
    return level


def noise(rng, shape, spread, limit, split=(), kind=jnp.bfloat16):
    drawn = jax.random.normal(rng, shape, jnp.float32) * spread
    if len(split) > 0:
        drawn = shard_levels(rng, shape, split, -0.22, 0.18) * drawn
    return jnp.clip(drawn, min=-limit, max=limit).astype(kind)


def setup_inputs(seed: int = 0, part: int = 0) -> dict:
    seeds = jax.random.split(jax.random.key(seed), 7)
    part_splits = jax.random.split(jax.random.fold_in(seeds[6], part), 7)
    return {
        "sources": noise(part_splits[0], (TOKENS, D), 1.0, 6.0, ((0, 16),)),
        "errors": noise(part_splits[1], (TARGETS, TOKENS, D), 1.0, 6.0, ((1, 16),)),
        "enc_weight": noise(seeds[2], (D, LATENTS), D ** -0.5, 0.125, ((1, 16),)),
        "enc_bias": noise(seeds[3], (LATENTS,), 0.5, 3.0, ((0, 16),), jnp.float32),
        "dec_weight": noise(seeds[4], (TARGETS, LATENTS, D), (LATENTS // 8) ** -0.5, 0.1875, ((1, 16),)),
        "active": touch_ends((jax.random.randint(part_splits[5], (TOKENS, LATENTS), 0, 3) < 1).astype(jnp.int32), jax.random.fold_in(part_splits[5], 1), 0, 1),
    }


def reference(sources, errors, enc_weight, enc_bias, dec_weight, active):
    pre = jnp.dot(sources, enc_weight, preferred_element_type=jnp.float32) + enc_bias.astype(jnp.float32)
    flags = active.astype(jnp.float32)
    codes = (pre * flags).astype(jnp.bfloat16)
    grads = []
    code_grad = jnp.zeros(pre.shape, jnp.float32)
    for target in range(TARGETS):
        grads.append(jnp.dot(codes.T, errors[target], preferred_element_type=jnp.float32))
        code_grad = code_grad + jnp.dot(errors[target], dec_weight[target].T, preferred_element_type=jnp.float32)
    dec_grad = jnp.stack(grads, 0)
    pre_grad = (code_grad * flags).astype(jnp.bfloat16)
    enc_grad = jnp.dot(sources.T, pre_grad, preferred_element_type=jnp.float32)
    input_grad = jnp.dot(pre_grad, enc_weight.T, preferred_element_type=jnp.float32)
    return code_grad, dec_grad, enc_grad, input_grad
```

```python
import jax
import jax.numpy as jnp
from jax import lax
from jax.sharding import PartitionSpec as P

BF = jnp.bfloat16
F32 = jnp.float32


def general(sources, errors, enc_weight, enc_bias, dec_weight, active):
    mine = lax.axis_index("tsec")
    rows_all = lax.all_gather(sources, "lat", axis=0, tiled=True)
    flags = active.astype(F32)
    share = rows_all.shape[0] // lax.axis_size("tsec")
    partial_value = jnp.dot(rows_all, enc_weight, preferred_element_type=F32)
    pre = lax.psum(partial_value, "tsec") + enc_bias
    codes = (pre * flags).astype(BF)
    targets = lax.all_gather(errors, "lat", axis=1, tiled=True)
    dec_grad = jnp.einsum("rl,trd->tld", codes, targets, preferred_element_type=F32)
    partial_code = jnp.einsum("trd,tld->rl", targets, dec_weight, preferred_element_type=F32)
    total = lax.psum(partial_code, "tsec")
    pre_grad = (total * flags).astype(BF)
    code_grad = lax.dynamic_slice_in_dim(total, mine * share, share, 0)
    enc_grad = jnp.einsum("rd,rl->dl", rows_all, pre_grad, preferred_element_type=F32)
    input_grad = lax.psum_scatter(
        jnp.einsum("rl,dl->rd", pre_grad, enc_weight, preferred_element_type=F32),
        "lat",
        scatter_dimension=0,
        tiled=True,
    )
    return (code_grad, dec_grad, enc_grad, input_grad)


NZ, NY, NC = 4, 2, 2


def swap(x, partner):
    pairs = []
    for z in range(NZ):
        for y in range(NY):
            for c in range(NC):
                pz, py, pc = partner(z, y, c)
                pairs.append(((z * NY + y) * NC + c, (pz * NY + py) * NC + pc))
    return lax.ppermute(x, "lat", pairs)


def over_core(x):
    return swap(x, lambda z, y, c: (z, y, 1 - c))


def over_y(x):
    return swap(x, lambda z, y, c: (z, 1 - y, c))


def over_mirror(x):
    return swap(x, lambda z, y, c: (NZ - 1 - z, y, c))


def over_pair(x):
    return swap(x, lambda z, y, c: (z ^ 1, y, c))


def gather(x):
    m = over_mirror(x)
    p = over_pair(x)
    q = over_pair(m)
    blocks = []
    for v in (x, m, p, q):
        half = jnp.concatenate([v, over_y(v)], 0)
        blocks.append(jnp.concatenate([half, over_core(half)], 0))
    return blocks


def grid(sources, errors, enc_weight, enc_bias, dec_weight, active):
    rows = sources.shape[0]
    i = lax.axis_index("lat")
    z, y, c = i // (NY * NC), (i // NC) % NY, i % NC
    zs = (z, NZ - 1 - z, z ^ 1, NZ - 1 - (z ^ 1))
    parts = ((y, c), (1 - y, c), (y, 1 - c), (1 - y, 1 - c))
    place = [[((zz * NY + yy) * NC + cc) * rows for yy, cc in parts] for zz in zs]

    weight_peer = over_core(enc_weight)
    errs = gather(errors[0])
    srcs = gather(sources)
    code_grad = jnp.zeros(active.shape, F32)
    grads, flags, keeps, sends = [], [], [], []
    for j in range(NZ):
        total = lax.dot_general(
            errs[j], dec_weight[0], (((1,), (1,)), ((), ())), preferred_element_type=F32
        )
        act = jnp.concatenate(
            [lax.dynamic_slice_in_dim(active, r, rows, 0) for r in place[j]], 0
        ).astype(F32)
        flags.append(act)
        for n, r in enumerate(place[j]):
            code_grad = lax.dynamic_update_slice_in_dim(
                code_grad, total[n * rows : (n + 1) * rows], r, 0
            )
        grad = (total * act).astype(BF)
        grads.append(grad)
        peer = over_core(grad[2 * rows :])
        nt = (((1,), (1,)), ((), ()))
        term = lax.dot_general(
            grad[: 2 * rows], enc_weight, nt, preferred_element_type=F32
        ) + lax.dot_general(peer, weight_peer, nt, preferred_element_type=F32)
        keeps.append(term[:rows] + over_y(term[rows:].astype(BF)).astype(F32))
    own = keeps[0] + over_pair(keeps[2].astype(BF)).astype(F32)
    far = keeps[1] + over_pair(keeps[3].astype(BF)).astype(F32)
    input_grad = own + over_mirror(far.astype(BF)).astype(F32)

    src = jnp.concatenate(srcs, 0)
    pre = jnp.dot(src, enc_weight, preferred_element_type=F32) + enc_bias
    codes = (pre * jnp.concatenate(flags, 0)).astype(BF)
    tn = (((0,), (0,)), ((), ()))
    dec_grad = lax.dot_general(
        codes, jnp.concatenate(errs, 0), tn, preferred_element_type=F32
    )
    enc_grad = lax.dot_general(
        src, jnp.concatenate(grads, 0), tn, preferred_element_type=F32
    )
    return code_grad, dec_grad[None], enc_grad, input_grad


def solution(mesh):
    on_grid = mesh.shape["lat"] == NZ * NY * NC and mesh.shape["tsec"] == 1
    return jax.shard_map(
        grid if on_grid else general,
        mesh=mesh,
        in_specs=(
            P(("grp", "lat"), "tsec"),
            P("tsec", ("grp", "lat"), None),
            P("tsec", "lat"),
            P("lat"),
            P("tsec", "lat", None),
            P("grp", "lat"),
        ),
        out_specs=(
            P(("grp", "tsec"), "lat"),
            P("tsec", ("grp", "lat"), None),
            P(("grp", "tsec"), "lat"),
            P(("grp", "lat"), "tsec"),
        ),
        check_vma=False,
    )
```

```python
import jax
import jax.numpy as jnp
from jax import lax
from jax.experimental import pallas as pl
from jax.experimental.pallas import tpu as pltpu
from jax.sharding import PartitionSpec as P

BF = jnp.bfloat16
F32 = jnp.float32


def general(sources, errors, enc_weight, enc_bias, dec_weight, active):
    mine = lax.axis_index("tsec")
    rows_all = lax.all_gather(sources, "lat", axis=0, tiled=True)
    flags = active.astype(F32)
    share = rows_all.shape[0] // lax.axis_size("tsec")
    partial_value = jnp.dot(rows_all, enc_weight, preferred_element_type=F32)
    pre = lax.psum(partial_value, "tsec") + enc_bias
    codes = (pre * flags).astype(BF)
    targets = lax.all_gather(errors, "lat", axis=1, tiled=True)
    dec_grad = jnp.einsum("rl,trd->tld", codes, targets, preferred_element_type=F32)
    partial_code = jnp.einsum("trd,tld->rl", targets, dec_weight, preferred_element_type=F32)
    total = lax.psum(partial_code, "tsec")
    pre_grad = (total * flags).astype(BF)
    code_grad = lax.dynamic_slice_in_dim(total, mine * share, share, 0)
    enc_grad = jnp.einsum("rd,rl->dl", rows_all, pre_grad, preferred_element_type=F32)
    input_grad = lax.psum_scatter(
        jnp.einsum("rl,dl->rd", pre_grad, enc_weight, preferred_element_type=F32),
        "lat",
        scatter_dimension=0,
        tiled=True,
    )
    return (code_grad, dec_grad, enc_grad, input_grad)


NZ, NY, NC = 4, 2, 2


def swap(x, partner):
    pairs = []
    for z in range(NZ):
        for y in range(NY):
            for c in range(NC):
                pz, py, pc = partner(z, y, c)
                pairs.append(((z * NY + y) * NC + c, (pz * NY + py) * NC + pc))
    return lax.ppermute(x, "lat", pairs)


def over_core(x):
    return swap(x, lambda z, y, c: (z, y, 1 - c))


def over_y(x):
    return swap(x, lambda z, y, c: (z, 1 - y, c))


def over_mirror(x):
    return swap(x, lambda z, y, c: (NZ - 1 - z, y, c))


def over_pair(x):
    return swap(x, lambda z, y, c: (z ^ 1, y, c))


VMEM = pl.BlockSpec(memory_space=pltpu.VMEM)
ANY = pl.BlockSpec(memory_space=pl.ANY)
PARAMS = pltpu.CompilerParams(vmem_limit_bytes=40 * 2**20)
NT = (((1,), (1,)), ((), ()))
NN = (((1,), (0,)), ((), ()))
TN = (((0,), (0,)), ((), ()))


def dot(a, b, dims):
    return lax.dot_general(a, b, dims, preferred_element_type=F32)


def like(shape, kind):
    return jax.ShapeDtypeStruct(shape, kind)


def call(kernel, outs, flops, *args, **options):
    moved = sum(a.size * a.dtype.itemsize for a in args)
    return pl.pallas_call(
        kernel,
        out_shape=outs,
        in_specs=options.pop("in_specs", [VMEM] * len(args)),
        out_specs=options.pop("out_specs", [VMEM] * len(outs)),
        compiler_params=PARAMS,
        cost_estimate=pl.CostEstimate(flops=1, bytes_accessed=1, transcendentals=0),
        **options,
    )(*args)


def flags_kernel(rows, place, active, flags, stage, sems):
    copies = [
        pltpu.make_async_copy(
            active.at[pl.ds(pl.multiple_of(place[n], rows), rows)],
            stage.at[pl.ds(n * rows, rows)],
            sems.at[n],
        )
        for n in range(NZ * NY * NC)
    ]
    for copy in copies:
        copy.start()
    for n, copy in enumerate(copies):
        copy.wait()
        span = pl.ds(n * rows, rows)
        flags[span] = stage[span].astype(F32)


def make_flags(place, active, rows):
    n = NZ * NY * NC
    return call(
        lambda *refs: flags_kernel(rows, *refs),
        [like(active.shape, F32)],
        active.size,
        place,
        active,
        in_specs=[pl.BlockSpec(memory_space=pltpu.SMEM), ANY],
        scratch_shapes=[pltpu.VMEM(active.shape, active.dtype), pltpu.SemaphoreType.DMA((n,))],
    )[0]


def place_kernel(rows, place, *refs):
    totals, out, sems = refs[:NZ], refs[NZ], refs[NZ + 1]
    copies = []
    for n in range(NZ * NY * NC):
        j, k = divmod(n, NY * NC)
        copies.append(
            pltpu.make_async_copy(
                totals[j].at[pl.ds(k * rows, rows)],
                out.at[pl.ds(pl.multiple_of(place[n], rows), rows)],
                sems.at[n],
            )
        )
    for copy in copies:
        copy.start()
    for copy in copies:
        copy.wait()


def place_rows(place, totals, rows):
    n = NZ * NY * NC
    return call(
        lambda *refs: place_kernel(rows, *refs),
        [like((n * rows, totals[0].shape[1]), F32)],
        0,
        place,
        *totals,
        in_specs=[pl.BlockSpec(memory_space=pltpu.SMEM)] + [VMEM] * NZ,
        out_specs=[ANY],
        scratch_shapes=[pltpu.SemaphoreType.DMA((n,))],
    )[0]


def code_kernel(j, half, *refs):
    *others, weight, flags, errs, total, grad = refs
    n = half.shape[0]
    errs[:n] = half[...]
    row = n
    for other in others:
        errs[row : row + other.shape[0]] = other[...]
        row += other.shape[0]
    value = dot(errs[...], weight[...], NT)
    total[...] = value
    grad[...] = (value * flags[pl.ds(j * 2 * n, 2 * n)]).astype(BF)


def code_step(j, half, others, weight, flags):
    n, d = half.shape
    lat = weight.shape[0]
    return call(
        lambda *refs: code_kernel(j, *refs),
        [like((2 * n, d), BF), like((2 * n, lat), F32), like((2 * n, lat), BF)],
        4 * n * d * lat,
        half,
        *others,
        weight,
        flags,
    )


def term_kernel(grad, peer, weight, weight_peer, keep, send):
    n = peer.shape[0]
    term = dot(grad[:n], weight[...], NT) + dot(peer[...], weight_peer[...], NT)
    keep[...] = term[: n // 2]
    send[...] = term[n // 2 :].astype(BF)


def term_step(grad, peer, weight, weight_peer):
    n, lat = peer.shape
    d = weight.shape[0]
    return call(
        term_kernel,
        [like((n // 2, d), F32), like((n // 2, d), BF)],
        4 * n * d * lat,
        grad,
        peer,
        weight,
        weight_peer,
    )


def pre_kernel(j, half, *refs):
    *others, weight, bias, flags, srcs, codes = refs
    n = half.shape[0]
    srcs[:n] = half[...]
    row = n
    for other in others:
        srcs[row : row + other.shape[0]] = other[...]
        row += other.shape[0]
    value = dot(srcs[...], weight[...], NN) + bias[...]
    codes[...] = (value * flags[pl.ds(j * 2 * n, 2 * n)]).astype(BF)


def pre_step(j, half, others, weight, bias, flags):
    n, d = half.shape
    lat = weight.shape[1]
    return call(
        lambda *refs: pre_kernel(j, *refs),
        [like((2 * n, d), BF), like((2 * n, lat), BF)],
        4 * n * d * lat,
        half,
        *others,
        weight,
        bias,
        flags,
    )


def tokens_kernel(*refs):
    codes, errs, srcs, grads = (refs[NZ * k : NZ * k + NZ] for k in range(4))
    dec_grad, enc_grad, token, turned = refs[4 * NZ + 1 :]
    token[...] = jnp.zeros_like(token)
    n, tile = codes[0].shape[0], enc_grad.shape[0]

    @pl.when(pl.program_id(0) == 0)
    def _():
        for j in range(NZ):
            turned[:, j * n : (j + 1) * n] = codes[j][...].T

    cols = pl.ds(pl.multiple_of(pl.program_id(0) * tile, tile), tile)
    dec_grad[...] = sum(
        dot(turned[:, j * n : (j + 1) * n], errs[j][:, cols], NN) for j in range(NZ)
    )
    enc_grad[...] = sum(dot(srcs[j][:, cols], grads[j][...], TN) for j in range(NZ))


def tokens_step(codes, errs, srcs, grads, last, tile=256):
    n, lat = codes[0].shape
    d = errs[0].shape[1]
    return call(
        tokens_kernel,
        [like((lat, d), F32), like((d, lat), F32), like((8, 128), F32)],
        4 * NZ * n * d * lat,
        *codes,
        *errs,
        *srcs,
        *grads,
        last,
        grid=(d // tile,),
        out_specs=[
            pl.BlockSpec((lat, tile), lambda t: (0, t)),
            pl.BlockSpec((tile, lat), lambda t: (t, 0)),
            VMEM,
        ],
        scratch_shapes=[pltpu.VMEM((lat, NZ * n), BF)],
    )


def after_kernel(x, *refs):
    refs[-1][...] = x[...]


def after(x, *others):
    return call(after_kernel, [like(x.shape, x.dtype)], 0, x, *others)[0]


def finish_kernel(keep, back, pair, top, bottom, token, out):
    n = top.shape[0]
    own = keep[...] + back[...].astype(F32) + pair[...].astype(F32)
    out[:n] = own[:n] + top[...].astype(F32)
    out[n:] = own[n:] + bottom[...].astype(F32)


def pack_kernel(count, *refs):
    row = 0
    for part in refs[:count]:
        n = part.shape[0]
        refs[-1][row : row + n] = part[...]
        row += n


def pack(parts, *others):
    n = sum(part.shape[0] for part in parts)
    out = like((n, parts[0].shape[1]), parts[0].dtype)
    return call(lambda *refs: pack_kernel(len(parts), *refs), [out], 0, *parts, *others)[0]


def pieces(send, x, count=2):
    n = x.shape[0] // count
    return [send(x[k * n : (k + 1) * n]) for k in range(count)]


def grid(sources, errors, enc_weight, enc_bias, dec_weight, active):
    rows = sources.shape[0]
    i = lax.axis_index("lat")
    z, y, c = i // (NY * NC), (i // NC) % NY, i % NC
    zs = (z, NZ - 1 - z, z ^ 1, NZ - 1 - (z ^ 1))
    parts = ((y, c), (1 - y, c), (y, 1 - c), (1 - y, 1 - c))
    place = jnp.stack([((zz * NY + yy) * NC + cc) * rows for zz in zs for yy, cc in parts])
    bias = enc_bias[None]
    flags = make_flags(place, active, rows)

    def code(j, half, others):
        return code_step(j, half, others, dec_weight[0], flags)

    def across(grad):
        return over_core(grad[2 * rows :])

    def term(grad, peer):
        return term_step(grad, peer, enc_weight, weight_peer)

    def plus(keep, *backs):
        n = keep.shape[0] // len(backs[0])
        return [
            keep[k * n : (k + 1) * n] + sum(back[k].astype(F32) for back in backs)
            for k in range(len(backs[0]))
        ]

    def pre(j, half, others):
        return pre_step(j, half, others, enc_weight, bias, flags)

    x, s = errors[0], sources
    y0, m, p = over_y(x), over_mirror(x), over_pair(x)
    s_y0, s_m = over_y(s), over_mirror(s)
    weight_peer = over_core(enc_weight)
    m = after(m, y0, p, flags, weight_peer)
    y1, q = pieces(over_y, m), pieces(over_pair, m)
    half0 = pack([x, y0], m, s_y0)
    other0 = pieces(over_core, half0)
    s_x = pack([s, s_y0], half0)
    s_other0 = pieces(over_core, s_x)
    errs0, total0, grad0 = code(0, half0, other0)
    q1 = [over_pair(after(part, grad0)) for part in y1]
    p = after(p, y1[0], grad0)
    y2 = pieces(over_y, p)
    half1 = pack([m, *y1], grad0, *q)
    other1, peer0 = pieces(over_core, half1, 4), across(after(grad0, half1))
    errs1, total1, grad1 = code(1, half1, other1)
    keep0, send0 = term(grad0, peer0)
    srcs0, codes0 = pre(0, s_x, [after(s_other0[0], grad1), s_other0[1]])
    half3 = pack([*q, *q1], send0, codes0, s_m)
    half2 = pack([p, *y2], half3)
    other3, other2 = pieces(over_core, half3), pieces(over_core, half2)
    back0, peer1 = over_y(after(send0, half3)), across(after(grad1, half3))
    s_m = after(s_m, half3)
    s_y1, s_q = over_y(s_m), over_pair(s_m)
    s_p = over_pair(after(s_x, half3))
    errs3, total3, grad3 = code(3, half3, other3)
    peer3 = across(grad3)
    errs2, total2, grad2 = code(2, after(half2, grad3), other2)
    peer2 = across(grad2)
    keep3, send3 = term(grad3, after(peer3, grad2))
    back3 = pieces(over_y, send3)
    keep1, send1 = term(after(grad1, send3), peer1)
    back1 = pieces(over_y, send1)
    keep2, send2 = term(after(grad2, send1, back0), peer2)
    back2 = over_y(send2)
    s_q = after(s_q, send2)
    s_y3 = over_y(s_q)
    s_m = pack([s_m, s_y1], send2)
    s_other1 = pieces(over_core, s_m)
    sum3 = [after(part.astype(BF), send2) for part in plus(keep3, back3)]
    pair3 = [over_pair(part) for part in sum3]
    s_p = after(s_p, *sum3)
    s_other2 = pieces(over_core, s_p)
    srcs1, codes1 = pre(1, s_m, [after(s_other1[0], *sum3), s_other1[1]])
    srcs2, codes2 = pre(2, s_p, s_other2)
    far = [part.astype(BF) for part in plus(keep1, back1, pair3)]
    far = [after(part, codes1, codes2) for part in far]
    far_in = [over_mirror(part) for part in far]
    sum2 = (keep2 + back2.astype(F32)).astype(BF)
    pair2 = over_pair(sum2)
    s_q = pack([s_q, s_y3], *far)
    srcs3, codes3 = pre(3, s_q, pieces(over_core, s_q))
    code_grad = place_rows(
        place, (total0, total1, total2, after(total3, *far)), rows
    )
    dec_grad, enc_grad, token = tokens_step(
        (codes0, codes1, codes2, codes3),
        (errs0, errs1, errs2, errs3),
        (srcs0, srcs1, srcs2, srcs3),
        (grad0, grad1, grad2, grad3),
        far[1],
    )
    input_grad = call(
        finish_kernel, [like(x.shape, F32)], 0, keep0, back0, pair2, *far_in, token
    )[0]
    return code_grad, dec_grad[None], enc_grad, input_grad


def solution(mesh):
    on_grid = mesh.shape["lat"] == NZ * NY * NC and mesh.shape["tsec"] == 1
    return jax.shard_map(
        grid if on_grid else general,
        mesh=mesh,
        in_specs=(
            P(("grp", "lat"), "tsec"),
            P("tsec", ("grp", "lat"), None),
            P("tsec", "lat"),
            P("lat"),
            P("tsec", "lat", None),
            P("grp", "lat"),
        ),
        out_specs=(
            P(("grp", "tsec"), "lat"),
            P("tsec", ("grp", "lat"), None),
            P(("grp", "tsec"), "lat"),
            P(("grp", "lat"), "tsec"),
        ),
        check_vma=False,
    )
```

```python
import jax
import jax.numpy as jnp
from jax import lax
from jax.experimental import pallas as pl
from jax.experimental.pallas import tpu as pltpu
from jax.sharding import PartitionSpec as P

BF = jnp.bfloat16
F32 = jnp.float32


def general(sources, errors, enc_weight, enc_bias, dec_weight, active):
    mine = lax.axis_index("tsec")
    rows_all = lax.all_gather(sources, "lat", axis=0, tiled=True)
    flags = active.astype(F32)
    share = rows_all.shape[0] // lax.axis_size("tsec")
    partial_value = jnp.dot(rows_all, enc_weight, preferred_element_type=F32)
    pre = lax.psum(partial_value, "tsec") + enc_bias
    codes = (pre * flags).astype(BF)
    targets = lax.all_gather(errors, "lat", axis=1, tiled=True)
    dec_grad = jnp.einsum("rl,trd->tld", codes, targets, preferred_element_type=F32)
    partial_code = jnp.einsum("trd,tld->rl", targets, dec_weight, preferred_element_type=F32)
    total = lax.psum(partial_code, "tsec")
    pre_grad = (total * flags).astype(BF)
    code_grad = lax.dynamic_slice_in_dim(total, mine * share, share, 0)
    enc_grad = jnp.einsum("rd,rl->dl", rows_all, pre_grad, preferred_element_type=F32)
    input_grad = lax.psum_scatter(
        jnp.einsum("rl,dl->rd", pre_grad, enc_weight, preferred_element_type=F32),
        "lat",
        scatter_dimension=0,
        tiled=True,
    )
    return (code_grad, dec_grad, enc_grad, input_grad)


NZ, NY, NC = 4, 2, 2


def swap(x, partner):
    pairs = []
    for z in range(NZ):
        for y in range(NY):
            for c in range(NC):
                pz, py, pc = partner(z, y, c)
                pairs.append(((z * NY + y) * NC + c, (pz * NY + py) * NC + pc))
    return lax.ppermute(x, "lat", pairs)


def over_core(x):
    return swap(x, lambda z, y, c: (z, y, 1 - c))


def over_y(x):
    return swap(x, lambda z, y, c: (z, 1 - y, c))


def over_mirror(x):
    return swap(x, lambda z, y, c: (NZ - 1 - z, y, c))


def over_pair(x):
    return swap(x, lambda z, y, c: (z ^ 1, y, c))


VMEM = pl.BlockSpec(memory_space=pltpu.VMEM)
ANY = pl.BlockSpec(memory_space=pl.ANY)
PARAMS = pltpu.CompilerParams(vmem_limit_bytes=16 * 2**20)
NT = (((1,), (1,)), ((), ()))
NN = (((1,), (0,)), ((), ()))
TN = (((0,), (0,)), ((), ()))


def dot(a, b, dims):
    return lax.dot_general(a, b, dims, preferred_element_type=F32)


def like(shape, kind):
    return jax.ShapeDtypeStruct(shape, kind)


def call(kernel, outs, flops, *args, **options):
    moved = sum(a.size * a.dtype.itemsize for a in args)
    return pl.pallas_call(
        kernel,
        out_shape=outs,
        in_specs=options.pop("in_specs", [VMEM] * len(args)),
        out_specs=options.pop("out_specs", [VMEM] * len(outs)),
        compiler_params=PARAMS,
        cost_estimate=pl.CostEstimate(flops=1, bytes_accessed=1, transcendentals=0),
        **options,
    )(*args)


def flags_kernel(rows, place, active, flags, stage, sems):
    copies = [
        pltpu.make_async_copy(
            active.at[pl.ds(pl.multiple_of(place[n], rows), rows)],
            stage.at[pl.ds(n * rows, rows)],
            sems.at[n],
        )
        for n in range(NZ * NY * NC)
    ]
    for copy in copies:
        copy.start()
    for n, copy in enumerate(copies):
        copy.wait()
        span = pl.ds(n * rows, rows)
        flags[span] = stage[span].astype(F32)


def make_flags(place, active, rows):
    n = NZ * NY * NC
    return call(
        lambda *refs: flags_kernel(rows, *refs),
        [like(active.shape, F32)],
        active.size,
        place,
        active,
        in_specs=[pl.BlockSpec(memory_space=pltpu.SMEM), ANY],
        scratch_shapes=[pltpu.VMEM(active.shape, active.dtype), pltpu.SemaphoreType.DMA((n,))],
    )[0]


def place_kernel(rows, place, *refs):
    totals, out, sems = refs[:NZ], refs[NZ], refs[NZ + 1]
    copies = []
    for n in range(NZ * NY * NC):
        j, k = divmod(n, NY * NC)
        copies.append(
            pltpu.make_async_copy(
                totals[j].at[pl.ds(k * rows, rows)],
                out.at[pl.ds(pl.multiple_of(place[n], rows), rows)],
                sems.at[n],
            )
        )
    for copy in copies:
        copy.start()
    for copy in copies:
        copy.wait()


def place_rows(place, totals, rows):
    n = NZ * NY * NC
    return call(
        lambda *refs: place_kernel(rows, *refs),
        [like((n * rows, totals[0].shape[1]), F32)],
        0,
        place,
        *totals,
        in_specs=[pl.BlockSpec(memory_space=pltpu.SMEM)] + [VMEM] * NZ,
        out_specs=[ANY],
        scratch_shapes=[pltpu.SemaphoreType.DMA((n,))],
    )[0]


def code_kernel(j, half, *refs):
    *others, weight, flags, errs, total, grad = refs
    n = half.shape[0]
    errs[:n] = half[...]
    row = n
    for other in others:
        errs[row : row + other.shape[0]] = other[...]
        row += other.shape[0]
    value = dot(errs[...], weight[...], NT)
    total[...] = value
    grad[...] = (value * flags[pl.ds(j * 2 * n, 2 * n)]).astype(BF)


def code_step(j, half, others, weight, flags):
    n, d = half.shape
    lat = weight.shape[0]
    return call(
        lambda *refs: code_kernel(j, *refs),
        [like((2 * n, d), BF), like((2 * n, lat), F32), like((2 * n, lat), BF)],
        4 * n * d * lat,
        half,
        *others,
        weight,
        flags,
    )


def term_kernel(grad, peer, weight, weight_peer, keep, send):
    n = peer.shape[0]
    term = dot(grad[:n], weight[...], NT) + dot(peer[...], weight_peer[...], NT)
    keep[...] = term[: n // 2]
    send[...] = term[n // 2 :].astype(BF)


def term_step(grad, peer, weight, weight_peer):
    n, lat = peer.shape
    d = weight.shape[0]
    return call(
        term_kernel,
        [like((n // 2, d), F32), like((n // 2, d), BF)],
        4 * n * d * lat,
        grad,
        peer,
        weight,
        weight_peer,
    )


def pre_kernel(j, half, *refs):
    *others, weight, bias, flags, srcs, codes = refs
    n = half.shape[0]
    srcs[:n] = half[...]
    row = n
    for other in others:
        srcs[row : row + other.shape[0]] = other[...]
        row += other.shape[0]
    value = dot(srcs[...], weight[...], NN) + bias[...]
    codes[...] = (value * flags[pl.ds(j * 2 * n, 2 * n)]).astype(BF)


def pre_step(j, half, others, weight, bias, flags):
    n, d = half.shape
    lat = weight.shape[1]
    return call(
        lambda *refs: pre_kernel(j, *refs),
        [like((2 * n, d), BF), like((2 * n, lat), BF)],
        4 * n * d * lat,
        half,
        *others,
        weight,
        bias,
        flags,
    )


def early_kernel(*refs):
    count = (len(refs) - 3) // 4
    codes, errs, srcs, grads = (refs[count * k : count * (k + 1)] for k in range(4))
    dec_grad, enc_grad, turned = refs[4 * count :]
    n, tile = codes[0].shape[0], 256
    for j in range(count):
        turned[:, j * n : (j + 1) * n] = codes[j][...].T

    @pl.loop(0, errs[0].shape[1] // tile)
    def _(t):
        cols = pl.ds(pl.multiple_of(t * tile, tile), tile)
        dec_grad[:, cols] = sum(
            dot(turned[:, j * n : (j + 1) * n], errs[j][:, cols], NN) for j in range(count)
        )
        enc_grad[cols, :] = sum(dot(srcs[j][:, cols], grads[j][...], TN) for j in range(count))


def early_step(codes, errs, srcs, grads):
    n, lat = codes[0].shape
    d = errs[0].shape[1]
    return call(
        early_kernel,
        [like((lat, d), F32), like((d, lat), F32)],
        1,
        *codes,
        *errs,
        *srcs,
        *grads,
        scratch_shapes=[pltpu.VMEM((lat, len(codes) * n), BF)],
    )


def late_kernel(*refs):
    count = (len(refs) - 6) // 4
    codes, errs, srcs, grads = (refs[count * k : count * (k + 1)] for k in range(4))
    dec_part, enc_part, dec_grad, enc_grad, token, turned = refs[4 * count :]
    token[...] = jnp.zeros_like(token)
    n, tile = codes[0].shape[0], enc_grad.shape[0]

    @pl.when(pl.program_id(0) == 0)
    def _():
        for j in range(count):
            turned[:, j * n : (j + 1) * n] = codes[j][...].T

    cols = pl.ds(pl.multiple_of(pl.program_id(0) * tile, tile), tile)
    dec_grad[...] = dec_part[:, cols] + sum(
        dot(turned[:, j * n : (j + 1) * n], errs[j][:, cols], NN) for j in range(count)
    )
    enc_grad[...] = enc_part[cols, :] + sum(
        dot(srcs[j][:, cols], grads[j][...], TN) for j in range(count)
    )


def late_step(codes, errs, srcs, grads, dec_part, enc_part, tile=256):
    n, lat = codes[0].shape
    d = errs[0].shape[1]
    return call(
        late_kernel,
        [like((lat, d), F32), like((d, lat), F32), like((8, 128), F32)],
        1,
        *codes,
        *errs,
        *srcs,
        *grads,
        dec_part,
        enc_part,
        grid=(d // tile,),
        out_specs=[
            pl.BlockSpec((lat, tile), lambda t: (0, t)),
            pl.BlockSpec((tile, lat), lambda t: (t, 0)),
            VMEM,
        ],
        scratch_shapes=[pltpu.VMEM((lat, len(codes) * n), BF)],
    )


def after_kernel(x, *refs):
    refs[-1][...] = x[...]


def after(x, *others):
    return call(after_kernel, [like(x.shape, x.dtype)], 0, x, *others)[0]


def add_kernel(keep, back, *refs):
    refs[-1][...] = (keep[...] + back[...].astype(F32)).astype(refs[-1].dtype)


def add(keep, back, kind, *others):
    return call(add_kernel, [like(keep.shape, kind)], 0, keep, back, *others)[0]


def finish_kernel(own, pair, far, token, out):
    out[...] = own[...] + pair[...].astype(F32) + far[...].astype(F32)


def pack_kernel(spans, *refs):
    row = 0
    for ref, (start, n) in zip(refs, spans):
        refs[-1][row : row + n] = ref[start : start + n]
        row += n


def pack(parts, *others):
    parts = [part if isinstance(part, tuple) else (part, 0, part.shape[0]) for part in parts]
    spans = [part[1:] for part in parts]
    first = parts[0][0]
    out = like((sum(n for _, n in spans), first.shape[1]), first.dtype)
    arrays = [part[0] for part in parts]
    return call(lambda *refs: pack_kernel(spans, *refs), [out], 0, *arrays, *others)[0]


def pieces(send, x, count=2):
    n = x.shape[0] // count
    return [send(x[k * n : (k + 1) * n]) for k in range(count)]


def grid(sources, errors, enc_weight, enc_bias, dec_weight, active):
    rows = sources.shape[0]
    i = lax.axis_index("lat")
    z, y, c = i // (NY * NC), (i // NC) % NY, i % NC
    zs = (z, NZ - 1 - z, z ^ 1, NZ - 1 - (z ^ 1))
    parts = ((y, c), (1 - y, c), (y, 1 - c), (1 - y, 1 - c))
    place = jnp.stack([((zz * NY + yy) * NC + cc) * rows for zz in zs for yy, cc in parts])
    bias = enc_bias[None]
    flags = make_flags(place, active, rows)

    def code(j, half, others):
        return code_step(j, half, others, dec_weight[0], flags)

    def across(grad):
        return over_core(grad[2 * rows :])

    def term(grad, peer):
        return term_step(grad, peer, enc_weight, weight_peer)

    def plus(keep, *backs):
        n = keep.shape[0] // len(backs[0])
        return [
            keep[k * n : (k + 1) * n] + sum(back[k].astype(F32) for back in backs)
            for k in range(len(backs[0]))
        ]

    def pre(j, half, others):
        return pre_step(j, half, others, enc_weight, bias, flags)

    x, s = errors[0], sources
    m, p = over_mirror(x), over_pair(x)
    y0, s_y0 = over_y(x), over_y(s)
    weight_peer = over_core(enc_weight)
    m = after(m, y0, p, flags, weight_peer)
    y1, q = over_y(m), over_pair(m)
    s = after(s, m)
    s_p, s_m = over_pair(s), over_mirror(s)
    q1, y2 = over_pair(y1), over_y(after(p, y1))
    s_y2 = over_y(s_p)
    half0 = pack([x, y0, s, s_y0], y1)
    half3 = pack([q, q1], s_m, s_y2, y2)
    other3 = over_core(half3)
    halves = pack([half0, m, y1, p, y2], half3)
    others = over_core(halves)
    s_m = after(s_m, half3)
    s_y1, s_q = over_y(s_m), over_pair(s_m)
    errs3, total3, grad3 = code(3, half3, [other3])
    peer3 = across(grad3)
    errs1, total1, grad1 = code(1, halves[4 * rows : 6 * rows], [after(others[4 * rows : 6 * rows], grad3)])
    keep3, send3 = term(grad3, after(peer3, grad1, s_y1, s_q))
    back3 = over_y(send3)
    errs2, total2, grad2 = code(2, halves[6 * rows :], [after(others[6 * rows :], send3)])
    peer1, peer2 = across(grad1), across(grad2)
    keep1, send1 = term(after(grad1, send3), peer1)
    back1 = over_y(send1)
    keep2, send2 = term(after(grad2, send1), peer2)
    back2 = over_y(send2)
    sum3 = after((keep3 + back3.astype(F32)).astype(BF), send1)
    pair3 = over_pair(sum3)
    s_q = after(s_q, sum3)
    s_y3 = over_y(s_q)
    s_mp = pack([s_m, s_y1, s_p, s_y2], sum3)
    s_other = over_core(s_mp)
    errs0, total0, grad0 = code(0, halves[: 2 * rows], [after(others[: 2 * rows], sum3)])
    keep0, send0 = term(grad0, across(grad0))
    back0 = over_y(send0)
    far = pack([(keep1 + back1.astype(F32) + pair3.astype(F32)).astype(BF)], send2)
    far_in = over_mirror(far)
    srcs0, codes0 = pre(0, halves[2 * rows : 4 * rows], [after(others[2 * rows : 4 * rows], far)])
    srcs1, codes1 = pre(1, s_mp[: 2 * rows], [after(s_other[: 2 * rows], far)])
    srcs2, codes2 = pre(2, s_mp[2 * rows :], [after(s_other[2 * rows :], far)])
    dec_part, enc_part = early_step(
        (codes0, codes1, codes2), (errs0, errs1, errs2), (srcs0, srcs1, srcs2), (grad0, grad1, grad2)
    )
    sum2 = add(keep2, back2, BF, codes1)
    pair2 = over_pair(sum2)
    own = add(keep0, back0, F32, dec_part)
    s_q = pack([s_q, s_y3], dec_part)
    cuts = (0, 3 * rows // 4, 3 * rows // 2, 2 * rows)
    q_other = [over_core(s_q[a:b]) for a, b in zip(cuts, cuts[1:])]
    srcs3, codes3 = pre(3, s_q, q_other)
    code_grad = place_rows(place, (total0, total1, total2, after(total3, dec_part)), rows)
    dec_grad, enc_grad, token = late_step(
        (codes3,), (errs3,), (srcs3,), (grad3,), dec_part, enc_part
    )
    input_grad = call(
        finish_kernel, [like(x.shape, F32)], 0, own, pair2, far_in, token
    )[0]
    return code_grad, dec_grad[None], enc_grad, input_grad


def solution(mesh):
    on_grid = mesh.shape["lat"] == NZ * NY * NC and mesh.shape["tsec"] == 1
    return jax.shard_map(
        grid if on_grid else general,
        mesh=mesh,
        in_specs=(
            P(("grp", "lat"), "tsec"),
            P("tsec", ("grp", "lat"), None),
            P("tsec", "lat"),
            P("lat"),
            P("tsec", "lat", None),
            P("grp", "lat"),
        ),
        out_specs=(
            P(("grp", "tsec"), "lat"),
            P("tsec", ("grp", "lat"), None),
            P(("grp", "tsec"), "lat"),
            P(("grp", "lat"), "tsec"),
        ),
        check_vma=False,
    )
```

```python
import jax
import jax.numpy as jnp
from jax import lax
from jax.experimental import pallas as pl
from jax.experimental.pallas import tpu as pltpu
from jax.sharding import PartitionSpec as P

BF = jnp.bfloat16
F32 = jnp.float32


def general(sources, errors, enc_weight, enc_bias, dec_weight, active):
    mine = lax.axis_index("tsec")
    rows_all = lax.all_gather(sources, "lat", axis=0, tiled=True)
    flags = active.astype(F32)
    share = rows_all.shape[0] // lax.axis_size("tsec")
    partial_value = jnp.dot(rows_all, enc_weight, preferred_element_type=F32)
    pre = lax.psum(partial_value, "tsec") + enc_bias
    codes = (pre * flags).astype(BF)
    targets = lax.all_gather(errors, "lat", axis=1, tiled=True)
    dec_grad = jnp.einsum("rl,trd->tld", codes, targets, preferred_element_type=F32)
    partial_code = jnp.einsum("trd,tld->rl", targets, dec_weight, preferred_element_type=F32)
    total = lax.psum(partial_code, "tsec")
    pre_grad = (total * flags).astype(BF)
    code_grad = lax.dynamic_slice_in_dim(total, mine * share, share, 0)
    enc_grad = jnp.einsum("rd,rl->dl", rows_all, pre_grad, preferred_element_type=F32)
    input_grad = lax.psum_scatter(
        jnp.einsum("rl,dl->rd", pre_grad, enc_weight, preferred_element_type=F32),
        "lat",
        scatter_dimension=0,
        tiled=True,
    )
    return (code_grad, dec_grad, enc_grad, input_grad)


NZ, NY, NC = 4, 2, 2


def swap(x, partner):
    pairs = []
    for z in range(NZ):
        for y in range(NY):
            for c in range(NC):
                pz, py, pc = partner(z, y, c)
                pairs.append(((z * NY + y) * NC + c, (pz * NY + py) * NC + pc))
    return lax.ppermute(x, "lat", pairs)


def over_core(x):
    return swap(x, lambda z, y, c: (z, y, 1 - c))


def over_y(x):
    return swap(x, lambda z, y, c: (z, 1 - y, c))


def over_mirror(x):
    return swap(x, lambda z, y, c: (NZ - 1 - z, y, c))


def over_pair(x):
    return swap(x, lambda z, y, c: (z ^ 1, y, c))


VMEM = pl.BlockSpec(memory_space=pltpu.VMEM)
ANY = pl.BlockSpec(memory_space=pl.ANY)
PARAMS = pltpu.CompilerParams(vmem_limit_bytes=16 * 2**20)
NT = (((1,), (1,)), ((), ()))
NN = (((1,), (0,)), ((), ()))
TN = (((0,), (0,)), ((), ()))


def dot(a, b, dims):
    return lax.dot_general(a, b, dims, preferred_element_type=F32)


def like(shape, kind):
    return jax.ShapeDtypeStruct(shape, kind)


def call(kernel, outs, flops, *args, **options):
    moved = sum(a.size * a.dtype.itemsize for a in args)
    return pl.pallas_call(
        kernel,
        out_shape=outs,
        in_specs=options.pop("in_specs", [VMEM] * len(args)),
        out_specs=options.pop("out_specs", [VMEM] * len(outs)),
        compiler_params=PARAMS,
        cost_estimate=pl.CostEstimate(flops=1, bytes_accessed=1, transcendentals=0),
        **options,
    )(*args)


def flags_kernel(rows, place, active, flags, stage, sems):
    copies = [
        pltpu.make_async_copy(
            active.at[pl.ds(pl.multiple_of(place[n], rows), rows)],
            stage.at[pl.ds(n * rows, rows)],
            sems.at[n],
        )
        for n in range(NZ * NY * NC)
    ]
    for copy in copies:
        copy.start()
    for n, copy in enumerate(copies):
        copy.wait()
        span = pl.ds(n * rows, rows)
        flags[span] = stage[span].astype(F32)


def make_flags(place, active, rows):
    n = NZ * NY * NC
    return call(
        lambda *refs: flags_kernel(rows, *refs),
        [like(active.shape, F32)],
        active.size,
        place,
        active,
        in_specs=[pl.BlockSpec(memory_space=pltpu.SMEM), ANY],
        scratch_shapes=[pltpu.VMEM(active.shape, active.dtype), pltpu.SemaphoreType.DMA((n,))],
    )[0]


def place_kernel(rows, place, *refs):
    totals, out, sems = refs[:NZ], refs[NZ], refs[NZ + 1]
    copies = []
    for n in range(NZ * NY * NC):
        j, k = divmod(n, NY * NC)
        copies.append(
            pltpu.make_async_copy(
                totals[j].at[pl.ds(k * rows, rows)],
                out.at[pl.ds(pl.multiple_of(place[n], rows), rows)],
                sems.at[n],
            )
        )
    for copy in copies:
        copy.start()
    for copy in copies:
        copy.wait()


def place_rows(place, totals, rows):
    n = NZ * NY * NC
    return call(
        lambda *refs: place_kernel(rows, *refs),
        [like((n * rows, totals[0].shape[1]), F32)],
        0,
        place,
        *totals,
        in_specs=[pl.BlockSpec(memory_space=pltpu.SMEM)] + [VMEM] * NZ,
        out_specs=[ANY],
        scratch_shapes=[pltpu.SemaphoreType.DMA((n,))],
    )[0]


def code_kernel(j, half, *refs):
    *others, weight, flags, errs, total, grad = refs
    n = half.shape[0]
    errs[:n] = half[...]
    row = n
    for other in others:
        errs[row : row + other.shape[0]] = other[...]
        row += other.shape[0]
    value = dot(errs[...], weight[...], NT)
    total[...] = value
    grad[...] = (value * flags[pl.ds(j * 2 * n, 2 * n)]).astype(BF)


def code_step(j, half, others, weight, flags):
    n, d = half.shape
    lat = weight.shape[0]
    return call(
        lambda *refs: code_kernel(j, *refs),
        [like((2 * n, d), BF), like((2 * n, lat), F32), like((2 * n, lat), BF)],
        4 * n * d * lat,
        half,
        *others,
        weight,
        flags,
    )


def term_kernel(grad, peer, weight, weight_peer, keep, send):
    n = peer.shape[0]
    term = dot(grad[:n], weight[...], NT) + dot(peer[...], weight_peer[...], NT)
    keep[...] = term[: n // 2]
    send[...] = term[n // 2 :].astype(BF)


def term_step(grad, peer, weight, weight_peer):
    n, lat = peer.shape
    d = weight.shape[0]
    return call(
        term_kernel,
        [like((n // 2, d), F32), like((n // 2, d), BF)],
        4 * n * d * lat,
        grad,
        peer,
        weight,
        weight_peer,
    )


def pre_kernel(j, half, *refs):
    *others, weight, bias, flags, srcs, codes = refs
    n = half.shape[0]
    srcs[:n] = half[...]
    row = n
    for other in others:
        srcs[row : row + other.shape[0]] = other[...]
        row += other.shape[0]
    value = dot(srcs[...], weight[...], NN) + bias[...]
    codes[...] = (value * flags[pl.ds(j * 2 * n, 2 * n)]).astype(BF)


def pre_step(j, half, others, weight, bias, flags):
    n, d = half.shape
    lat = weight.shape[1]
    return call(
        lambda *refs: pre_kernel(j, *refs),
        [like((2 * n, d), BF), like((2 * n, lat), BF)],
        4 * n * d * lat,
        half,
        *others,
        weight,
        bias,
        flags,
    )


def early_kernel(*refs):
    count = (len(refs) - 3) // 4
    codes, errs, srcs, grads = (refs[count * k : count * (k + 1)] for k in range(4))
    dec_grad, enc_grad, turned = refs[4 * count :]
    n, tile = codes[0].shape[0], 896
    for j in range(count):
        turned[:, j * n : (j + 1) * n] = codes[j][...].T

    @pl.loop(0, errs[0].shape[1] // tile)
    def _(t):
        cols = pl.ds(pl.multiple_of(t * tile, tile), tile)
        dec_grad[:, cols] = sum(
            dot(turned[:, j * n : (j + 1) * n], errs[j][:, cols], NN) for j in range(count)
        )
        enc_grad[cols, :] = sum(dot(srcs[j][:, cols], grads[j][...], TN) for j in range(count))


def early_step(codes, errs, srcs, grads):
    n, lat = codes[0].shape
    d = errs[0].shape[1]
    return call(
        early_kernel,
        [like((lat, d), F32), like((d, lat), F32)],
        1,
        *codes,
        *errs,
        *srcs,
        *grads,
        scratch_shapes=[pltpu.VMEM((lat, len(codes) * n), BF)],
    )


def late_kernel(*refs):
    count = (len(refs) - 6) // 4
    codes, errs, srcs, grads = (refs[count * k : count * (k + 1)] for k in range(4))
    dec_part, enc_part, dec_grad, enc_grad, token, turned = refs[4 * count :]
    token[...] = jnp.zeros_like(token)
    n, tile = codes[0].shape[0], enc_grad.shape[0]

    @pl.when(pl.program_id(0) == 0)
    def _():
        for j in range(count):
            turned[:, j * n : (j + 1) * n] = codes[j][...].T

    cols = pl.ds(pl.multiple_of(pl.program_id(0) * tile, tile), tile)
    dec_grad[...] = dec_part[:, cols] + sum(
        dot(turned[:, j * n : (j + 1) * n], errs[j][:, cols], NN) for j in range(count)
    )
    enc_grad[...] = enc_part[cols, :] + sum(
        dot(srcs[j][:, cols], grads[j][...], TN) for j in range(count)
    )


def late_step(codes, errs, srcs, grads, dec_part, enc_part, tile=256):
    n, lat = codes[0].shape
    d = errs[0].shape[1]
    return call(
        late_kernel,
        [like((lat, d), F32), like((d, lat), F32), like((8, 128), F32)],
        1,
        *codes,
        *errs,
        *srcs,
        *grads,
        dec_part,
        enc_part,
        grid=(d // tile,),
        out_specs=[
            pl.BlockSpec((lat, tile), lambda t: (0, t)),
            pl.BlockSpec((tile, lat), lambda t: (t, 0)),
            VMEM,
        ],
        scratch_shapes=[pltpu.VMEM((lat, len(codes) * n), BF)],
    )


def after_kernel(x, *refs):
    refs[-1][...] = x[...]


def after(x, *others):
    return call(after_kernel, [like(x.shape, x.dtype)], 0, x, *others)[0]


def add_kernel(keep, back, *refs):
    refs[-1][...] = (keep[...] + back[...].astype(F32)).astype(refs[-1].dtype)


def add(keep, back, kind, *others):
    return call(add_kernel, [like(keep.shape, kind)], 0, keep, back, *others)[0]


def finish_kernel(own, pair, far, token, out):
    out[...] = own[...] + pair[...].astype(F32) + far[...].astype(F32)


def pack_kernel(spans, *refs):
    row = 0
    for ref, (start, n) in zip(refs, spans):
        refs[-1][row : row + n] = ref[start : start + n]
        row += n


def pack(parts, *others):
    parts = [part if isinstance(part, tuple) else (part, 0, part.shape[0]) for part in parts]
    spans = [part[1:] for part in parts]
    first = parts[0][0]
    out = like((sum(n for _, n in spans), first.shape[1]), first.dtype)
    arrays = [part[0] for part in parts]
    return call(lambda *refs: pack_kernel(spans, *refs), [out], 0, *arrays, *others)[0]


def pieces(send, x, count=2):
    n = x.shape[0] // count
    return [send(x[k * n : (k + 1) * n]) for k in range(count)]


def grid(sources, errors, enc_weight, enc_bias, dec_weight, active):
    rows = sources.shape[0]
    i = lax.axis_index("lat")
    z, y, c = i // (NY * NC), (i // NC) % NY, i % NC
    zs = (z, NZ - 1 - z, z ^ 1, NZ - 1 - (z ^ 1))
    parts = ((y, c), (1 - y, c), (y, 1 - c), (1 - y, 1 - c))
    place = jnp.stack([((zz * NY + yy) * NC + cc) * rows for zz in zs for yy, cc in parts])
    bias = enc_bias[None]
    flags = make_flags(place, active, rows)

    def code(j, half, others):
        return code_step(j, half, others, dec_weight[0], flags)

    def across(grad):
        return over_core(grad[2 * rows :])

    def term(grad, peer):
        return term_step(grad, peer, enc_weight, weight_peer)

    def plus(keep, *backs):
        n = keep.shape[0] // len(backs[0])
        return [
            keep[k * n : (k + 1) * n] + sum(back[k].astype(F32) for back in backs)
            for k in range(len(backs[0]))
        ]

    def pre(j, half, others):
        return pre_step(j, half, others, enc_weight, bias, flags)

    x, s = errors[0], sources
    m, p = over_mirror(x), over_pair(x)
    y0, s_y0 = over_y(x), over_y(s)
    weight_peer = over_core(enc_weight)
    m = after(m, y0, p, flags, weight_peer)
    y1, q = over_y(m), over_pair(m)
    s = after(s, m)
    s_m = over_mirror(s)
    q1, y2 = over_pair(y1), over_y(after(p, y1))
    s_p = over_pair(after(s, y1))
    half3 = pack([q, q1], s_m, y2)
    other3 = over_core(half3)
    halves = pack([x, y0, s, s_y0, m, y1, p, y2], half3)
    others = over_core(halves)
    s_m = after(s_m, half3)
    s_y1 = over_y(s_m)
    s_q, s_p1 = over_pair(s_m), over_pair(after(s_y0, half3))
    errs3, total3, grad3 = code(3, half3, [other3])
    peer3 = across(grad3)
    errs1, total1, grad1 = code(1, halves[4 * rows : 6 * rows], [after(others[4 * rows : 6 * rows], grad3)])
    keep3, send3 = term(grad3, after(peer3, grad1, s_y1, s_p))
    back3 = over_y(send3)
    errs2, total2, grad2 = code(2, halves[6 * rows :], [after(others[6 * rows :], send3)])
    peer1, peer2 = across(grad1), across(grad2)
    keep1, send1 = term(after(grad1, send3), peer1)
    back1 = over_y(send1)
    keep2, send2 = term(after(grad2, send1), peer2)
    back2 = over_y(send2)
    sum3 = after((keep3 + back3.astype(F32)).astype(BF), send1, s_q)
    pair3 = over_pair(sum3)
    s_q = after(s_q, sum3)
    s_y3 = over_y(s_q)
    s_mp = pack([s_m, s_y1, s_p, s_p1], sum3)
    s_other = over_core(s_mp)
    errs0, total0, grad0 = code(0, halves[: 2 * rows], [after(others[: 2 * rows], sum3)])
    keep0, send0 = term(grad0, across(grad0))
    back0 = over_y(send0)
    far = pack([(keep1 + back1.astype(F32) + pair3.astype(F32)).astype(BF)], send2)
    far_in = over_mirror(far)
    srcs0, codes0 = pre(0, halves[2 * rows : 4 * rows], [after(others[2 * rows : 4 * rows], sum3)])
    srcs1, codes1 = pre(1, s_mp[: 2 * rows], [after(s_other[: 2 * rows], sum3)])
    srcs2, codes2 = pre(2, s_mp[2 * rows :], [after(s_other[2 * rows :], sum3)])
    dec_part, enc_part = early_step(
        (after(codes0, far), codes1, codes2), (errs0, errs1, errs2), (srcs0, srcs1, srcs2), (grad0, grad1, grad2)
    )
    sum2 = add(keep2, back2, BF, codes1)
    pair2 = over_pair(sum2)
    own = add(keep0, back0, F32, dec_part)
    s_q = pack([s_q, s_y3], dec_part)
    cuts = (0, 3 * rows // 4, 3 * rows // 2, 2 * rows)
    q_other = [over_core(s_q[a:b]) for a, b in zip(cuts, cuts[1:])]
    srcs3, codes3 = pre(3, s_q, q_other)
    code_grad = place_rows(place, (total0, total1, total2, after(total3, dec_part)), rows)
    dec_grad, enc_grad, token = late_step(
        (codes3,), (errs3,), (srcs3,), (grad3,), dec_part, enc_part, 896
    )
    input_grad = call(
        finish_kernel, [like(x.shape, F32)], 0, own, pair2, far_in, token
    )[0]
    return code_grad, dec_grad[None], enc_grad, input_grad


def solution(mesh):
    on_grid = mesh.shape["lat"] == NZ * NY * NC and mesh.shape["tsec"] == 1
    return jax.shard_map(
        grid if on_grid else general,
        mesh=mesh,
        in_specs=(
            P(("grp", "lat"), "tsec"),
            P("tsec", ("grp", "lat"), None),
            P("tsec", "lat"),
            P("lat"),
            P("tsec", "lat", None),
            P("grp", "lat"),
        ),
        out_specs=(
            P(("grp", "tsec"), "lat"),
            P("tsec", ("grp", "lat"), None),
            P(("grp", "tsec"), "lat"),
            P(("grp", "lat"), "tsec"),
        ),
        check_vma=False,
    )
```

```python
import jax
import jax.numpy as jnp
from jax import lax
from jax.experimental import pallas as pl
from jax.experimental.pallas import tpu as pltpu
from jax.sharding import PartitionSpec as P

BF = jnp.bfloat16
F32 = jnp.float32


def general(sources, errors, enc_weight, enc_bias, dec_weight, active):
    mine = lax.axis_index("tsec")
    rows_all = lax.all_gather(sources, "lat", axis=0, tiled=True)
    flags = active.astype(F32)
    share = rows_all.shape[0] // lax.axis_size("tsec")
    partial_value = jnp.dot(rows_all, enc_weight, preferred_element_type=F32)
    pre = lax.psum(partial_value, "tsec") + enc_bias
    codes = (pre * flags).astype(BF)
    targets = lax.all_gather(errors, "lat", axis=1, tiled=True)
    dec_grad = jnp.einsum("rl,trd->tld", codes, targets, preferred_element_type=F32)
    partial_code = jnp.einsum("trd,tld->rl", targets, dec_weight, preferred_element_type=F32)
    total = lax.psum(partial_code, "tsec")
    pre_grad = (total * flags).astype(BF)
    code_grad = lax.dynamic_slice_in_dim(total, mine * share, share, 0)
    enc_grad = jnp.einsum("rd,rl->dl", rows_all, pre_grad, preferred_element_type=F32)
    input_grad = lax.psum_scatter(
        jnp.einsum("rl,dl->rd", pre_grad, enc_weight, preferred_element_type=F32),
        "lat",
        scatter_dimension=0,
        tiled=True,
    )
    return (code_grad, dec_grad, enc_grad, input_grad)


NZ, NY, NC = 4, 2, 2


def swap(x, partner):
    pairs = []
    for z in range(NZ):
        for y in range(NY):
            for c in range(NC):
                pz, py, pc = partner(z, y, c)
                pairs.append(((z * NY + y) * NC + c, (pz * NY + py) * NC + pc))
    return lax.ppermute(x, "lat", pairs)


def over_core(x):
    return swap(x, lambda z, y, c: (z, y, 1 - c))


def over_y(x):
    return swap(x, lambda z, y, c: (z, 1 - y, c))


def over_mirror(x):
    return swap(x, lambda z, y, c: (NZ - 1 - z, y, c))


def over_pair(x):
    return swap(x, lambda z, y, c: (z ^ 1, y, c))


VMEM = pl.BlockSpec(memory_space=pltpu.VMEM)
ANY = pl.BlockSpec(memory_space=pl.ANY)
PARAMS = pltpu.CompilerParams(vmem_limit_bytes=16 * 2**20)
NT = (((1,), (1,)), ((), ()))
NN = (((1,), (0,)), ((), ()))
TN = (((0,), (0,)), ((), ()))


def dot(a, b, dims):
    return lax.dot_general(a, b, dims, preferred_element_type=F32)


def like(shape, kind):
    return jax.ShapeDtypeStruct(shape, kind)


def call(kernel, outs, flops, *args, **options):
    moved = sum(a.size * a.dtype.itemsize for a in args)
    return pl.pallas_call(
        kernel,
        out_shape=outs,
        in_specs=options.pop("in_specs", [VMEM] * len(args)),
        out_specs=options.pop("out_specs", [VMEM] * len(outs)),
        compiler_params=PARAMS,
        cost_estimate=pl.CostEstimate(flops=1, bytes_accessed=1, transcendentals=0),
        **options,
    )(*args)


def flags_kernel(rows, place, active, flags, stage, sems):
    copies = [
        pltpu.make_async_copy(
            active.at[pl.ds(pl.multiple_of(place[n], rows), rows)],
            stage.at[pl.ds(n * rows, rows)],
            sems.at[n],
        )
        for n in range(NZ * NY * NC)
    ]
    for copy in copies:
        copy.start()
    for n, copy in enumerate(copies):
        copy.wait()
        span = pl.ds(n * rows, rows)
        flags[span] = stage[span].astype(F32)


def make_flags(place, active, rows):
    n = NZ * NY * NC
    return call(
        lambda *refs: flags_kernel(rows, *refs),
        [like(active.shape, F32)],
        active.size,
        place,
        active,
        in_specs=[pl.BlockSpec(memory_space=pltpu.SMEM), ANY],
        scratch_shapes=[pltpu.VMEM(active.shape, active.dtype), pltpu.SemaphoreType.DMA((n,))],
    )[0]


def place_kernel(rows, place, *refs):
    totals, out, sems = refs[:NZ], refs[NZ], refs[NZ + 1]
    copies = []
    for n in range(NZ * NY * NC):
        j, k = divmod(n, NY * NC)
        copies.append(
            pltpu.make_async_copy(
                totals[j].at[pl.ds(k * rows, rows)],
                out.at[pl.ds(pl.multiple_of(place[n], rows), rows)],
                sems.at[n],
            )
        )
    for copy in copies:
        copy.start()
    for copy in copies:
        copy.wait()


def place_rows(place, totals, rows):
    n = NZ * NY * NC
    return call(
        lambda *refs: place_kernel(rows, *refs),
        [like((n * rows, totals[0].shape[1]), F32)],
        0,
        place,
        *totals,
        in_specs=[pl.BlockSpec(memory_space=pltpu.SMEM)] + [VMEM] * NZ,
        out_specs=[ANY],
        scratch_shapes=[pltpu.SemaphoreType.DMA((n,))],
    )[0]


def code_kernel(j, half, *refs):
    *others, weight, flags, errs, total, grad = refs
    n = half.shape[0]
    errs[:n] = half[...]
    row = n
    for other in others:
        errs[row : row + other.shape[0]] = other[...]
        row += other.shape[0]
    value = dot(errs[...], weight[...], NT)
    total[...] = value
    grad[...] = (value * flags[pl.ds(j * 2 * n, 2 * n)]).astype(BF)


def code_step(j, half, others, weight, flags):
    n, d = half.shape
    lat = weight.shape[0]
    return call(
        lambda *refs: code_kernel(j, *refs),
        [like((2 * n, d), BF), like((2 * n, lat), F32), like((2 * n, lat), BF)],
        4 * n * d * lat,
        half,
        *others,
        weight,
        flags,
    )


def term_kernel(grad, peer, weight, weight_peer, keep, send):
    n = peer.shape[0]
    term = dot(grad[:n], weight[...], NT) + dot(peer[...], weight_peer[...], NT)
    keep[...] = term[: n // 2]
    send[...] = term[n // 2 :].astype(BF)


def term_step(grad, peer, weight, weight_peer):
    n, lat = peer.shape
    d = weight.shape[0]
    return call(
        term_kernel,
        [like((n // 2, d), F32), like((n // 2, d), BF)],
        4 * n * d * lat,
        grad,
        peer,
        weight,
        weight_peer,
    )


def pre_kernel(j, half, *refs):
    *others, weight, bias, flags, srcs, codes = refs
    n = half.shape[0]
    srcs[:n] = half[...]
    row = n
    for other in others:
        srcs[row : row + other.shape[0]] = other[...]
        row += other.shape[0]
    value = dot(srcs[...], weight[...], NN) + bias[...]
    codes[...] = (value * flags[pl.ds(j * 2 * n, 2 * n)]).astype(BF)


def pre_step(j, half, others, weight, bias, flags):
    n, d = half.shape
    lat = weight.shape[1]
    return call(
        lambda *refs: pre_kernel(j, *refs),
        [like((2 * n, d), BF), like((2 * n, lat), BF)],
        4 * n * d * lat,
        half,
        *others,
        weight,
        bias,
        flags,
    )


def early_kernel(*refs):
    count = (len(refs) - 3) // 4
    codes, errs, srcs, grads = (refs[count * k : count * (k + 1)] for k in range(4))
    dec_grad, enc_grad, turned = refs[4 * count :]
    n, tile = codes[0].shape[0], 896
    for j in range(count):
        turned[:, j * n : (j + 1) * n] = codes[j][...].T

    @pl.loop(0, errs[0].shape[1] // tile)
    def _(t):
        cols = pl.ds(pl.multiple_of(t * tile, tile), tile)
        dec_grad[:, cols] = sum(
            dot(turned[:, j * n : (j + 1) * n], errs[j][:, cols], NN) for j in range(count)
        )
        enc_grad[cols, :] = sum(dot(srcs[j][:, cols], grads[j][...], TN) for j in range(count))


def early_step(codes, errs, srcs, grads):
    n, lat = codes[0].shape
    d = errs[0].shape[1]
    return call(
        early_kernel,
        [like((lat, d), F32), like((d, lat), F32)],
        1,
        *codes,
        *errs,
        *srcs,
        *grads,
        scratch_shapes=[pltpu.VMEM((lat, len(codes) * n), BF)],
    )


def late_kernel(*refs):
    count = (len(refs) - 6) // 4
    codes, errs, srcs, grads = (refs[count * k : count * (k + 1)] for k in range(4))
    dec_part, enc_part, dec_grad, enc_grad, token, turned = refs[4 * count :]
    token[...] = jnp.zeros_like(token)
    n, tile = codes[0].shape[0], enc_grad.shape[0]

    @pl.when(pl.program_id(0) == 0)
    def _():
        for j in range(count):
            turned[:, j * n : (j + 1) * n] = codes[j][...].T

    cols = pl.ds(pl.multiple_of(pl.program_id(0) * tile, tile), tile)
    dec_grad[...] = dec_part[:, cols] + sum(
        dot(turned[:, j * n : (j + 1) * n], errs[j][:, cols], NN) for j in range(count)
    )
    enc_grad[...] = enc_part[cols, :] + sum(
        dot(srcs[j][:, cols], grads[j][...], TN) for j in range(count)
    )


def late_step(codes, errs, srcs, grads, dec_part, enc_part, tile=256):
    n, lat = codes[0].shape
    d = errs[0].shape[1]
    return call(
        late_kernel,
        [like((lat, d), F32), like((d, lat), F32), like((8, 128), F32)],
        1,
        *codes,
        *errs,
        *srcs,
        *grads,
        dec_part,
        enc_part,
        grid=(d // tile,),
        out_specs=[
            pl.BlockSpec((lat, tile), lambda t: (0, t)),
            pl.BlockSpec((tile, lat), lambda t: (t, 0)),
            VMEM,
        ],
        scratch_shapes=[pltpu.VMEM((lat, len(codes) * n), BF)],
    )


def after_kernel(x, *refs):
    refs[-1][...] = x[...]


def after(x, *others):
    return call(after_kernel, [like(x.shape, x.dtype)], 0, x, *others)[0]


def add_kernel(keep, back, *refs):
    refs[-1][...] = (keep[...] + back[...].astype(F32)).astype(refs[-1].dtype)


def add(keep, back, kind, *others):
    return call(add_kernel, [like(keep.shape, kind)], 0, keep, back, *others)[0]


def finish_kernel(own, pair, far, token, out):
    out[...] = own[...] + pair[...].astype(F32) + far[...].astype(F32)


def pack_kernel(spans, *refs):
    row = 0
    for ref, (start, n) in zip(refs, spans):
        refs[-1][row : row + n] = ref[start : start + n]
        row += n


def pack(parts, *others):
    parts = [part if isinstance(part, tuple) else (part, 0, part.shape[0]) for part in parts]
    spans = [part[1:] for part in parts]
    first = parts[0][0]
    out = like((sum(n for _, n in spans), first.shape[1]), first.dtype)
    arrays = [part[0] for part in parts]
    return call(lambda *refs: pack_kernel(spans, *refs), [out], 0, *arrays, *others)[0]


def pieces(send, x, count=2):
    n = x.shape[0] // count
    return [send(x[k * n : (k + 1) * n]) for k in range(count)]


def grid(sources, errors, enc_weight, enc_bias, dec_weight, active):
    rows = sources.shape[0]
    i = lax.axis_index("lat")
    z, y, c = i // (NY * NC), (i // NC) % NY, i % NC
    zs = (z, NZ - 1 - z, z ^ 1, NZ - 1 - (z ^ 1))
    parts = ((y, c), (1 - y, c), (y, 1 - c), (1 - y, 1 - c))
    place = jnp.stack([((zz * NY + yy) * NC + cc) * rows for zz in zs for yy, cc in parts])
    bias = enc_bias[None]
    flags = make_flags(place, active, rows)

    def code(j, half, others):
        return code_step(j, half, others, dec_weight[0], flags)

    def across(grad):
        return over_core(grad[2 * rows :])

    def term(grad, peer):
        return term_step(grad, peer, enc_weight, weight_peer)

    def plus(keep, *backs):
        n = keep.shape[0] // len(backs[0])
        return [
            keep[k * n : (k + 1) * n] + sum(back[k].astype(F32) for back in backs)
            for k in range(len(backs[0]))
        ]

    def pre(j, half, others):
        return pre_step(j, half, others, enc_weight, bias, flags)

    x, s = errors[0], sources
    m, p = over_mirror(x), over_pair(x)
    y0, s_y0 = over_y(x), over_y(s)
    weight_peer = over_core(enc_weight)
    m = after(m, y0, p, flags, weight_peer)
    y1, q = over_y(m), over_pair(m)
    s = after(s, m)
    s_m = over_mirror(s)
    q1, y2 = over_pair(y1), over_y(after(p, y1))
    s_p = over_pair(after(s, y1))
    half3 = pack([q, q1], s_m, y2)
    other3 = over_core(half3)
    halves = pack([x, y0, s, s_y0, m, y1, p, y2], half3)
    others = over_core(halves)
    s_m = after(s_m, half3)
    s_y1 = over_y(s_m)
    s_q, s_p1 = over_pair(s_m), over_pair(after(s_y0, half3))
    errs3, total3, grad3 = code(3, half3, [other3])
    peer3 = across(grad3)
    errs1, total1, grad1 = code(1, halves[4 * rows : 6 * rows], [after(others[4 * rows : 6 * rows], grad3)])
    errs0, total0, grad0 = code(0, halves[: 2 * rows], [after(others[: 2 * rows], grad1)])
    keep3, send3 = term(grad3, after(peer3, grad0, s_y1, s_p))
    back3 = over_y(send3)
    errs2, total2, grad2 = code(2, halves[6 * rows :], [after(others[6 * rows :], send3)])
    peer1, peer2 = across(grad1), across(grad2)
    keep1, send1 = term(after(grad1, send3), peer1)
    back1 = over_y(send1)
    keep2, send2 = term(after(grad2, send1), peer2)
    back2 = over_y(send2)
    sum3 = after((keep3 + back3.astype(F32)).astype(BF), send1, s_q)
    pair3 = over_pair(sum3)
    s_q = after(s_q, sum3)
    s_y3 = over_y(s_q)
    s_mp = pack([s_m, s_y1, s_p, s_p1], sum3)
    s_other = over_core(s_mp)
    keep0, send0 = term(after(grad0, sum3), across(grad0))
    back0 = over_y(send0)
    far = pack([(keep1 + back1.astype(F32) + pair3.astype(F32)).astype(BF)], send2)
    far_in = over_mirror(far)
    srcs0, codes0 = pre(0, halves[2 * rows : 4 * rows], [after(others[2 * rows : 4 * rows], sum3)])
    srcs1, codes1 = pre(1, s_mp[: 2 * rows], [after(s_other[: 2 * rows], sum3)])
    srcs2, codes2 = pre(2, s_mp[2 * rows :], [after(s_other[2 * rows :], sum3)])
    dec_part, enc_part = early_step(
        (after(codes0, far), codes1, codes2), (errs0, errs1, errs2), (srcs0, srcs1, srcs2), (grad0, grad1, grad2)
    )
    sum2 = add(keep2, back2, BF, codes1)
    pair2 = over_pair(sum2)
    own = add(keep0, back0, F32, dec_part)
    s_q = pack([s_q, s_y3], dec_part)
    cuts = (0, 3 * rows // 4, 3 * rows // 2, 2 * rows)
    q_other = [over_core(s_q[a:b]) for a, b in zip(cuts, cuts[1:])]
    srcs3, codes3 = pre(3, s_q, q_other)
    code_grad = place_rows(place, (total0, total1, total2, after(total3, dec_part)), rows)
    dec_grad, enc_grad, token = late_step(
        (codes3,), (errs3,), (srcs3,), (grad3,), dec_part, enc_part, 896
    )
    input_grad = call(
        finish_kernel, [like(x.shape, F32)], 0, own, pair2, far_in, token
    )[0]
    return code_grad, dec_grad[None], enc_grad, input_grad


def solution(mesh):
    on_grid = mesh.shape["lat"] == NZ * NY * NC and mesh.shape["tsec"] == 1
    return jax.shard_map(
        grid if on_grid else general,
        mesh=mesh,
        in_specs=(
            P(("grp", "lat"), "tsec"),
            P("tsec", ("grp", "lat"), None),
            P("tsec", "lat"),
            P("lat"),
            P("tsec", "lat", None),
            P("grp", "lat"),
        ),
        out_specs=(
            P(("grp", "tsec"), "lat"),
            P("tsec", ("grp", "lat"), None),
            P(("grp", "tsec"), "lat"),
            P(("grp", "lat"), "tsec"),
        ),
        check_vma=False,
    )
```
